32 devices in a mesh: groups: 2 (over y), dp: 4 (over z), section: 4 (over x, core).
Axes of the slice: x: 2, y: 2, z: 4, core: 2. Of those that a mesh axis runs over, the one named last changes fastest.
Arguments:
- images: bfloat16 [4, 8, 16, 5120], P(None, ('groups', 'dp')), parts along dimension 1, may hold values from -40 to 40
- cotangent: bfloat16 [4, 8, 16, 5120], P(None, ('groups', 'dp')), parts along dimension 1, may hold values from -6 to 6
- in_weight: bfloat16 [4, 1280, 320], P('section'), may hold values from -0.3125 to 0.3125
- out_weight: bfloat16 [4, 1280, 320], P('section'), may hold values from -0.15625 to 0.15625
- depth_kernel: float32 [4, 49, 320], P('section'), may hold values from -0.875 to 0.875
- norm_gain: float32 [4, 320], P('section'), may hold values from 0.1 to 1.9
Outputs:
- input_grads: bfloat16 [4, 4, 8, 16, 5120], P('section', None, ('groups', 'dp')), parts along dimension 2
- in_weight_grad: float32 [8, 1280, 320], P(('groups', 'section'), 'dp'), parts along dimension 0
- out_weight_grad: float32 [8, 1280, 320], P(('groups', 'section'), 'dp'), parts along dimension 0
- kernel_grad: float32 [8, 49, 320], P(('groups', 'section')), parts along dimension 0
- gain_grad: float32 [8, 320], P(('groups', 'section')), parts along dimension 0
The draws below stay inside these ranges and needn't reach their ends.
There are 2 independent parts, one for each index of `groups`. The reference program is written for one: setup_inputs(seed, part) draws one part's arguments, and reference() takes and returns one part's arrays. A program takes and returns all parts, laid end to end along the dimension named above; an argument that names none is the same for every part. Nothing has to cross between parts.
All inputs are finite; a program needn't handle non-finite values.
Results may differ from the reference program's by a relative error of at most 0.015.
Values may be sent and summed in bfloat16 or wider, within the bound.
A program may use at most 64 MiB of HBM per device.

```python
import math
import jax
import jax.numpy as jnp
from jax import lax

C = 320
HID = 1280
KS = 7
MICRO = 4
TILE_H = 16
TILE_W = 16
IMAGES = 4
N_SECTION = 4


def draw_images(key, part):
    base_key, channel_key, pixel_key = jax.random.split(key, 3)
    spread = 0.5 * math.log(10.0)
    full_shape = (MICRO, IMAGES, TILE_H, TILE_W, C)
    channel_scale = jnp.exp(jax.random.uniform(channel_key, (C,), jnp.float32, -spread, spread))
    pixel_scale = jnp.exp(jax.random.uniform(pixel_key, (MICRO, IMAGES, TILE_H, TILE_W, 1), jnp.float32, -spread, spread))
    base_values = jnp.clip(jax.random.normal(base_key, full_shape, jnp.float32), -4.0, 4.0)
    scaled = base_values * channel_scale * pixel_scale
    return scaled.reshape(MICRO, IMAGES, TILE_H, TILE_W * C).astype(jnp.bfloat16)


def steps_of(key, dims, shards, smallest, top_value):
    level = 1.0
    for axis_at, shards_of in shards:
        heights = jax.random.uniform(jax.random.fold_in(jax.random.fold_in(key, 6), axis_at), (shards_of,), jnp.float32, smallest / len(shards), top_value / len(shards))
        level = level * jnp.repeat(jnp.exp(heights), dims[axis_at] // shards_of).reshape((-1,) + (1,) * (len(dims) - 1 - axis_at))
    return level


def scatter_about(rng, shape, scale, most, shards=(), kind=jnp.bfloat16):
    drawn = scale * jax.random.normal(rng, shape, jnp.float32)
    if shards:
        drawn = drawn * steps_of(rng, shape, shards, -0.22, 0.18)
    return jnp.clip(drawn, -most, most).astype(kind)


def setup_inputs(seed: int = 0, part: int = 0) -> dict:
    streams_of = jax.random.split(jax.random.key(seed), 7)
    part_splits = jax.random.split(jax.random.fold_in(streams_of[6], part), 7)
    return {
        "images": draw_images(jax.random.fold_in(jax.random.fold_in(streams_of[6], part), 71), part),
        "cotangent": scatter_about(part_splits[1], (MICRO, IMAGES, TILE_H, TILE_W * C), 1.0, 6.0, ((1, 4),)),
        "in_weight": scatter_about(streams_of[2], (N_SECTION, HID, C), C ** -0.5, 0.3125, ((0, 4),)),
        "out_weight": scatter_about(streams_of[3], (N_SECTION, HID, C), HID ** -0.5, 0.15625, ((0, 4),)),
        "depth_kernel": scatter_about(streams_of[4], (N_SECTION, KS * KS, C), (KS * KS) ** -0.5, 0.875, ((0, 4),), jnp.float32),
        "norm_gain": jnp.clip(1.0 + 0.18 * jax.random.normal(streams_of[5], (N_SECTION, C), jnp.float32), 0.1, 1.9),
    }


gelu_scale = 0.7978845608028654
cubic_term = 0.044715
norm_eps = 1e-06

def gelu_value(pre_act):
    tanh_val = jnp.tanh(gelu_scale * (pre_act + cubic_term * pre_act * pre_act * pre_act))
    return 0.5 * pre_act * (1.0 + tanh_val)

def gelu_slope(pre_act):
    tanh_val = jnp.tanh(gelu_scale * (pre_act + cubic_term * pre_act * pre_act * pre_act))
    inner_slope = gelu_scale * (1.0 + 3.0 * cubic_term * pre_act * pre_act)
    return 0.5 * (1.0 + tanh_val) + 0.5 * pre_act * (1.0 - tanh_val * tanh_val) * inner_slope

def depthwise(grid_field, kernel):
    kernel_reach = KS // 2
    tile_rows, tile_cols = (grid_field.shape[1], grid_field.shape[2])
    padded = jnp.pad(grid_field, ((0, 0), (kernel_reach, kernel_reach), (kernel_reach, kernel_reach), (0, 0)))
    accumulated = jnp.zeros_like(grid_field)
    for row_tap in range(KS):
        for col_tap in range(KS):
            accumulated = accumulated + padded[:, row_tap:row_tap + tile_rows, col_tap:col_tap + tile_cols, :] * kernel[row_tap * KS + col_tap]
    return accumulated

def depthwise_back(grad_field, kernel):
    kernel_reach = KS // 2
    tile_rows, tile_cols = (grad_field.shape[1], grad_field.shape[2])
    padded = jnp.pad(grad_field, ((0, 0), (kernel_reach, kernel_reach), (kernel_reach, kernel_reach), (0, 0)))
    accumulated = jnp.zeros_like(grad_field)
    for row_tap in range(KS):
        for col_tap in range(KS):
            row_from = 2 * kernel_reach - row_tap
            col_from = 2 * kernel_reach - col_tap
            accumulated = accumulated + padded[:, row_from:row_from + tile_rows, col_from:col_from + tile_cols, :] * kernel[row_tap * KS + col_tap]
    return accumulated

def kernel_terms(grid_field, grad_field):
    kernel_reach = KS // 2
    tile_rows, tile_cols = (grid_field.shape[1], grid_field.shape[2])
    padded = jnp.pad(grid_field, ((0, 0), (kernel_reach, kernel_reach), (kernel_reach, kernel_reach), (0, 0)))
    tap_sums = []
    for row_tap in range(KS):
        for col_tap in range(KS):
            window = padded[:, row_tap:row_tap + tile_rows, col_tap:col_tap + tile_cols, :]
            tap_sums.append(lax.optimization_barrier(jnp.sum(window * grad_field, axis=(0, 1, 2))))
    return jnp.stack(tap_sums)

def normalize(conv_out):
    average = lax.optimization_barrier(jnp.mean(conv_out, axis=-1, keepdims=True))
    centred = conv_out - average
    variance = lax.optimization_barrier(jnp.mean(centred * centred, axis=-1, keepdims=True))
    inv_std = lax.rsqrt(variance + norm_eps)
    return (centred * inv_std, inv_std)

def forward_block(block_in, weight_in, weight_out, kernel, gain_row):
    batch_size, tile_rows, flat_width = block_in.shape
    channels = weight_in.shape[1]
    grid_field = block_in.reshape(batch_size, tile_rows, flat_width // channels, channels).astype(jnp.float32)
    normalized, inv_std = normalize(depthwise(grid_field, kernel))
    normed = (normalized * gain_row).astype(jnp.bfloat16).reshape(-1, channels)
    pre_act = lax.dot_general(normed, weight_in, (((1,), (1,)), ((), ())), preferred_element_type=jnp.float32)
    hidden = gelu_value(pre_act).astype(jnp.bfloat16)
    mixed = jnp.dot(hidden, weight_out, preferred_element_type=jnp.float32)
    block_out = (grid_field.reshape(-1, channels) + mixed).astype(jnp.bfloat16)
    return (block_out.reshape(block_in.shape), pre_act)

def backward_block(block_in, pre_act, grad_out, weight_in, weight_out, kernel, gain_row, mean_scale):
    batch_size, tile_rows, flat_width = block_in.shape
    channels = weight_in.shape[1]
    grid_field = block_in.reshape(batch_size, tile_rows, flat_width // channels, channels).astype(jnp.float32)
    normalized, inv_std = normalize(depthwise(grid_field, kernel))
    flat_normal = normalized.reshape(-1, channels)
    flat_inv = inv_std.reshape(-1, 1)
    normed = (flat_normal * gain_row).astype(jnp.bfloat16)
    hidden = gelu_value(pre_act).astype(jnp.bfloat16)
    upstream = grad_out.reshape(-1, channels)
    contract_rows = (((0,), (0,)), ((), ()))
    out_term = lax.dot_general(hidden, upstream, contract_rows, preferred_element_type=jnp.float32) * mean_scale
    hidden_grad = lax.dot_general(upstream, weight_out, (((1,), (1,)), ((), ())), preferred_element_type=jnp.float32)
    act_grad = (hidden_grad * gelu_slope(pre_act)).astype(jnp.bfloat16)
    in_term = lax.dot_general(act_grad, normed, contract_rows, preferred_element_type=jnp.float32) * mean_scale
    normed_grad = jnp.dot(act_grad, weight_in, preferred_element_type=jnp.float32)
    gain_term = lax.optimization_barrier(jnp.sum(normed_grad * flat_normal, axis=0)) * mean_scale
    scaled = normed_grad * gain_row
    centred_grad = flat_inv * (scaled - lax.optimization_barrier(jnp.mean(scaled, axis=-1, keepdims=True)) - flat_normal * lax.optimization_barrier(jnp.mean(scaled * flat_normal, axis=-1, keepdims=True)))
    conv_grad = centred_grad.reshape(grid_field.shape)
    kernel_term = kernel_terms(grid_field, conv_grad) * mean_scale
    conv_back = depthwise_back(conv_grad, kernel).reshape(-1, channels)
    grad_in = (upstream.astype(jnp.float32) + conv_back).astype(jnp.bfloat16).reshape(block_in.shape)
    return (grad_in, normed, hidden, act_grad, upstream, (in_term, out_term, kernel_term, gain_term))

def reference(images, cotangent, in_weight, out_weight, depth_kernel, norm_gain):
    activation = images.reshape(MICRO * IMAGES, TILE_H, TILE_W * C)
    inputs = []
    for section_num in range(N_SECTION):
        inputs.append(activation)
        activation, unused_act = forward_block(activation, in_weight[section_num], out_weight[section_num], depth_kernel[section_num], norm_gain[section_num])
    grad_field = cotangent.reshape(MICRO * IMAGES, TILE_H, TILE_W * C)
    mean_scale = 1.0 / (MICRO * IMAGES)
    grads_list = [None] * N_SECTION
    in_list = [None] * N_SECTION
    out_list = [None] * N_SECTION
    kernel_list = [None] * N_SECTION
    gain_list = [None] * N_SECTION
    for section_num in reversed(range(N_SECTION)):
        unused_out, pre_act = forward_block(inputs[section_num], in_weight[section_num], out_weight[section_num], depth_kernel[section_num], norm_gain[section_num])
        grad_field, normed, hidden, act_grad, upstream, grad_terms = backward_block(inputs[section_num], pre_act, grad_field, in_weight[section_num], out_weight[section_num], depth_kernel[section_num], norm_gain[section_num], mean_scale)
        grads_list[section_num] = grad_field.reshape(MICRO, IMAGES, TILE_H, TILE_W * C)
        in_list[section_num] = grad_terms[0]
        out_list[section_num] = grad_terms[1]
        kernel_list[section_num] = grad_terms[2]
        gain_list[section_num] = grad_terms[3]
    return (jnp.stack(grads_list), jnp.stack(in_list), jnp.stack(out_list), jnp.stack(kernel_list), jnp.stack(gain_list))
```

```python
import functools

import jax
import jax.numpy as jnp
from jax import lax
from jax.experimental import pallas as pl
from jax.experimental.pallas import tpu as pltpu
from jax.sharding import PartitionSpec as P

KS = 7
REACH = KS // 2
LANES = 128
MESH = pl.DeviceIdType.MESH

gelu_scale = 0.7978845608028654
cubic_term = 0.044715
norm_eps = 1e-06
F32 = jnp.float32
BF16 = jnp.bfloat16


def half_turn(tile):
    return pltpu.roll(tile, LANES // 2, axis=tile.ndim - 1)


def low_lanes(tile):
    return lax.broadcasted_iota(jnp.int32, tile.shape, tile.ndim - 1) < LANES // 2


def split_pair(tiles):
    t0, t1, t2, t3, t4 = tiles
    low = low_lanes(t0)
    q2, q3, q4 = half_turn(t2), half_turn(t3), half_turn(t4)
    first = (t0, t1, jnp.where(low, t2, 0.0))
    second = (jnp.where(low, q2, q3), jnp.where(low, q3, q4), jnp.where(low, q4, 0.0))
    return first, second


def merge_pair(first, second):
    low = low_lanes(first[0])
    q0, q1, q2 = (half_turn(t) for t in second)
    return (
        first[0],
        first[1],
        jnp.where(low, first[2], q0),
        jnp.where(low, q0, q1),
        jnp.where(low, q1, q2),
    )


def lane_tiles(value):
    return tuple(value[:, k * LANES : (k + 1) * LANES] for k in range(value.shape[1] // LANES))


def from_native(ref, slot):
    rows, width = ref.shape[1], ref.shape[2]
    parts = []
    for pair in range(width // (5 * LANES)):
        value = ref[slot, :, pair * 5 * LANES : (pair + 1) * 5 * LANES].astype(F32)
        first, second = split_pair(lane_tiles(value))
        parts.append(jnp.concatenate(first, axis=1))
        parts.append(jnp.concatenate(second, axis=1))
    return jnp.concatenate(parts, axis=0)


def to_native(ref, slot, value):
    rows, width = ref.shape[1], ref.shape[2]
    for pair in range(width // (5 * LANES)):
        first = lane_tiles(value[2 * pair * rows : (2 * pair + 1) * rows])
        second = lane_tiles(value[(2 * pair + 1) * rows : (2 * pair + 2) * rows])
        for k, tile in enumerate(merge_pair(first, second)):
            at = (pair * 5 + k) * LANES
            ref[slot, :, at : at + LANES] = tile.astype(ref.dtype)


def put_padded(field, slot, value, rows):
    half = value.shape[0] // 2
    pairs = half // rows
    left, right = lane_tiles(value[:half]), lane_tiles(value[half:])
    body = merge_pair(left, right)
    edge = REACH * rows
    zeros = tuple(jnp.zeros((edge, LANES), F32) for _ in range(3))
    before = merge_pair(zeros, lane_tiles(value[half - edge : half]))
    after = lane_tiles(value[half : half + edge])
    for k in range(5):
        field[slot, k, REACH : REACH + pairs, 8 : 8 + rows, :] = body[k].reshape(pairs, rows, LANES)
        if k >= 2:
            field[slot, k, 0:REACH, 8 : 8 + rows, :] = before[k].reshape(REACH, rows, LANES)
        if k <= 2:
            field[slot, k, REACH + pairs :, 8 : 8 + rows, :] = after[k].reshape(REACH, rows, LANES)
    return body


def convolve(field, slot, taps, out, flip):
    pairs, rows = out.shape[1], out.shape[2]

    def one_tile(k, carry):
        for part in range(rows // 8):
            total = jnp.zeros((pairs, 8, LANES), F32)
            for i in range(KS):
                window = field[slot, k, :, 8 - REACH + i + 8 * part : 16 - REACH + i + 8 * part, :]
                for j in range(KS):
                    tap = KS * i + j
                    tap = KS * KS - 1 - tap if flip else tap
                    total = total + window[j : j + pairs] * taps[k, tap][None]
            out[k, :, 8 * part : 8 * part + 8, :] = total
        return carry

    lax.fori_loop(0, 5, one_tile, 0)
    tiles = tuple(out[k].reshape(pairs * rows, LANES) for k in range(5))
    first, second = split_pair(tiles)
    return jnp.concatenate(
        [jnp.concatenate(first, axis=1), jnp.concatenate(second, axis=1)], axis=0
    )


def tap_terms(field, slot, kept, sums):
    pairs, rows = kept.shape[2], kept.shape[3]

    def one_tile(k, carry):
        for i in range(KS):
            windows = [
                field[slot, k, :, 8 - REACH + i + 8 * part : 16 - REACH + i + 8 * part, :]
                for part in range(rows // 8)
            ]
            for j in range(KS):
                total = None
                for part in range(rows // 8):
                    term = jnp.sum(
                        windows[part][j : j + pairs]
                        * kept[slot, k, :, 8 * part : 8 * part + 8, :],
                        axis=0,
                    )
                    total = term if total is None else total + term
                tap = KS * KS - 1 - (KS * i + j)
                sums[k, tap] = sums[k, tap] + total
        return carry

    lax.fori_loop(0, 5, one_tile, 0)


def step_kernel(
    sections, replicas, spread, channels, mean_scale,
    images, cotangent, weight_in, weight_out, kernel, gain,
    stored, in_grad, out_grad, kernel_grad, gain_grad,
    x_in, x_out, g_in, win, wout, taps, wide, gain_wide,
    hidden, slope, act_grad, normed, upstream, unit, inv_std,
    field, kept, conv, tap_sums, gain_sums, sent, landed, small, small_in,
    load_sem, fwd_send, fwd_recv, bwd_send, bwd_recv, sum_send, sum_recv, small_send, small_recv,
):
    me = lax.axis_index("section")
    replica = lax.axis_index("dp")
    last = sections - 1
    micro_count, rows, width = x_in.shape
    hidden_width = weight_in.shape[0]
    step = 256
    chunks = hidden_width // step
    pixels = rows * (width // channels)

    barrier = pltpu.get_barrier_semaphore()

    @pl.when(me > 0)
    def _():
        pl.semaphore_signal(barrier, inc=1, device_id={"section": me - 1}, device_id_type=MESH)

    @pl.when(me < last)
    def _():
        pl.semaphore_signal(barrier, inc=1, device_id={"section": me + 1}, device_id_type=MESH)

    if spread:
        for k in range(1, replicas):
            pl.semaphore_signal(
                barrier, inc=1,
                device_id={"dp": lax.rem(replica + k, replicas)}, device_id_type=MESH,
            )

    def load(source, target, m, which):
        return pltpu.make_async_copy(source.at[m], target.at[m], load_sem.at[which, m])

    for m in range(micro_count):
        @pl.when(me == 0)
        def _():
            load(images, x_in, m, 0).start()

        @pl.when(me == last)
        def _():
            load(cotangent, g_in, m, 1).start()

    win[:, 256:384] = jnp.zeros((hidden_width, 128), BF16)
    wout[:, 256:384] = jnp.zeros((hidden_width, 128), BF16)
    win[:, 0:channels] = weight_in[...]
    wout[:, 0:channels] = weight_out[...]
    wide[...] = jnp.zeros(wide.shape, F32)
    gain_wide[...] = jnp.zeros(gain_wide.shape, F32)
    wide[0 : KS * KS, 0:channels] = kernel[...]
    gain_wide[:, 0:channels] = jnp.broadcast_to(gain[...], (8, channels))
    row_tiles = lane_tiles(wide[...])
    for k, tile in enumerate(merge_pair(row_tiles, row_tiles)):
        for t in range(KS * KS):
            taps[k, t] = jnp.broadcast_to(tile[t : t + 1], (8, LANES))
    field[...] = jnp.zeros(field.shape, F32)
    tap_sums[...] = jnp.zeros(tap_sums.shape, F32)
    gain_sums[...] = jnp.zeros(gain_sums.shape, F32)
    gain_row = gain_wide[0:1, :]

    neighbours = jnp.where(me > 0, 1, 0) + jnp.where(me < last, 1, 0)
    if spread:
        neighbours = neighbours + replicas - 1
    pl.semaphore_wait(barrier, neighbours)

    real = lax.broadcasted_iota(jnp.int32, (pixels, 384), 1) < channels
    by_channel = (((1,), (1,)), ((), ()))
    by_pixel = (((0,), (0,)), ((), ()))

    def ahead(m):
        return pltpu.make_async_remote_copy(
            src_ref=x_out.at[m], dst_ref=x_in.at[m],
            send_sem=fwd_send.at[m], recv_sem=fwd_recv.at[m],
            device_id={"section": jnp.minimum(me + 1, last)}, device_id_type=MESH,
        )

    def back(m):
        return pltpu.make_async_remote_copy(
            src_ref=stored.at[m], dst_ref=g_in.at[m],
            send_sem=bwd_send.at[m], recv_sem=bwd_recv.at[m],
            device_id={"section": jnp.maximum(me - 1, 0)}, device_id_type=MESH,
        )

    def forward(m, carry):
        @pl.when(me == 0)
        def _():
            load(images, x_in, m, 0).wait()

        @pl.when(me > 0)
        def _():
            ahead(m).wait_recv()

        x = from_native(x_in, m)
        body = put_padded(field, m, x, rows)
        for k in range(5):
            kept[m, k] = body[k].reshape(kept.shape[2:])
        u = convolve(field, m, taps, conv, False)
        mean = jnp.sum(u, axis=1, keepdims=True) * (1.0 / channels)
        centred = jnp.where(real, u - mean, 0.0)
        variance = jnp.sum(centred * centred, axis=1, keepdims=True) * (1.0 / channels)
        inverse = lax.rsqrt(variance + norm_eps)
        nhat = centred * inverse
        unit[m] = nhat
        inv_std[m] = jnp.broadcast_to(inverse, (pixels, LANES))
        n = (nhat * gain_row).astype(BF16)
        normed[m] = n
        mixed = None
        for c in range(chunks):
            at = slice(c * step, (c + 1) * step)
            a = lax.dot_general(n, win[at, :], by_channel, preferred_element_type=F32)
            square = a * a
            t = jnp.tanh(a * (gelu_scale + (gelu_scale * cubic_term) * square))
            plus = 0.5 + 0.5 * t
            h = (a * plus).astype(BF16)
            hidden[m, :, at] = h
            slope[m, :, at] = plus + (a * (plus * (1.0 - t))) * (
                gelu_scale + (3.0 * gelu_scale * cubic_term) * square
            )
            term = jnp.dot(h, wout[at, :], preferred_element_type=F32)
            mixed = term if mixed is None else mixed + term

        @pl.when(me < last)
        def _():
            to_native(x_out, m, x + mixed)
            ahead(m).start()

        return carry

    lax.fori_loop(0, micro_count, forward, 0)

    def backward(m, carry):
        @pl.when(me == last)
        def _():
            load(cotangent, g_in, m, 1).wait()

        @pl.when(me < last)
        def _():
            back(m).wait_recv()

        g = from_native(g_in, m)
        gb = g.astype(BF16)
        upstream[m] = gb
        dn = None
        for c in range(chunks):
            at = slice(c * step, (c + 1) * step)
            hg = lax.dot_general(gb, wout[at, :], by_channel, preferred_element_type=F32)
            da = (hg * slope[m, :, at]).astype(BF16)
            act_grad[m, :, at] = da
            term = jnp.dot(da, win[at, :], preferred_element_type=F32)
            dn = term if dn is None else dn + term
        nhat = unit[m]
        along = dn * nhat
        gain_sums[...] = gain_sums[...] + jnp.sum(along.reshape(pixels // 8, 8, 384), axis=0)
        q = dn * gain_row
        first = jnp.sum(q, axis=1, keepdims=True) * (1.0 / channels)
        second = jnp.sum(along * gain_row, axis=1, keepdims=True) * (1.0 / channels)
        du = jnp.where(real, inv_std[m][:, 0:1] * (q - first - nhat * second), 0.0)
        put_padded(field, m, du, rows)
        to_native(stored, m, g + convolve(field, m, taps, conv, True))

        @pl.when(me > 0)
        def _():
            back(m).start()

        return carry

    lax.fori_loop(0, micro_count, backward, 0)

    def share(w, k):
        chunk = hidden_width // replicas
        dest = lax.rem(replica + k, replicas)
        return pltpu.make_async_remote_copy(
            src_ref=sent.at[w, pl.ds(pl.multiple_of(dest * chunk, 16), chunk), :],
            dst_ref=landed.at[w, k - 1],
            send_sem=sum_send.at[w, k - 1], recv_sem=sum_recv.at[w, k - 1],
            device_id={"dp": dest}, device_id_type=MESH,
        )

    for w, (wide_side, thin_side) in enumerate(((hidden, upstream), (act_grad, normed))):
        for c in range(chunks):
            at = slice(c * step, (c + 1) * step)
            total = lax.dot_general(
                wide_side[:, :, at].reshape(micro_count * pixels, step),
                thin_side[...].reshape(micro_count * pixels, 384),
                by_pixel, preferred_element_type=F32,
            )
            total = (total[:, 0:channels] * mean_scale).astype(BF16)
            if spread:
                sent[w, at, :] = total
            elif w == 0:
                out_grad[at, :] = total
            else:
                in_grad[at, :] = total
        if spread:
            for k in range(1, replicas):
                share(w, k).start()

    def per_micro(m, carry):
        tap_terms(field, m, kept, tap_sums)
        return carry

    lax.fori_loop(0, micro_count, per_micro, 0)

    sums = tuple(jnp.sum(tap_sums[k], axis=1) for k in range(5))
    first, second = split_pair(sums)
    both = (jnp.concatenate(first, axis=1) + jnp.concatenate(second, axis=1)) * mean_scale
    gains = jnp.sum(gain_sums[...], axis=0, keepdims=True) * mean_scale
    if not spread:
        kernel_grad[...] = both[:, 0:channels]
        gain_grad[...] = gains[:, 0:channels]
    else:
        small[...] = jnp.zeros(small.shape, BF16)
        small[0:64, :] = jnp.concatenate(
            [both, jnp.zeros((15, 384), F32)], axis=0
        ).astype(BF16)
        small[64:80, :] = jnp.broadcast_to(gains, (16, 384)).astype(BF16)

        def share_small(k):
            return pltpu.make_async_remote_copy(
                src_ref=small, dst_ref=small_in.at[replica],
                send_sem=small_send.at[k - 1], recv_sem=small_recv.at[k - 1],
                device_id={"dp": lax.rem(replica + k, replicas)}, device_id_type=MESH,
            )

        for k in range(1, replicas):
            share_small(k).start()
        small_in[replica] = small[...]
        chunk = hidden_width // replicas
        mine = pl.ds(pl.multiple_of(replica * chunk, 16), chunk)
        for w, target in ((0, out_grad), (1, in_grad)):
            for k in range(1, replicas):
                share(w, k).wait()
            total = sent[w, mine, :].astype(F32)
            for k in range(1, replicas):
                total = total + landed[w, k - 1].astype(F32)
            target[...] = total
        for k in range(1, replicas):
            share_small(k).wait()
        total = small_in[0].astype(F32)
        for k in range(1, replicas):
            total = total + small_in[k].astype(F32)
        kernel_grad[...] = total[0 : KS * KS, 0:channels]
        gain_grad[...] = total[64:65, 0:channels]

    def drain(m, carry):
        @pl.when(me < last)
        def _():
            ahead(m).wait_send()

        @pl.when(me > 0)
        def _():
            back(m).wait_send()

        return carry

    lax.fori_loop(0, micro_count, drain, 0)


def local(images, cotangent, in_weight, out_weight, depth_kernel, norm_gain):
    sections = lax.axis_size("section")
    replicas = lax.axis_size("dp")
    micro_count, batch, rows, width = images.shape
    hidden_width, channels = in_weight.shape[1:]
    columns = width // channels
    pixels = rows * columns
    pairs = columns // 2
    assert batch == 1 and channels == 320 and rows % 8 == 0
    mean_scale = 1.0 / (micro_count * batch * replicas)
    chunk = hidden_width // replicas
    spread = chunk % 16 == 0 and replicas <= 8
    grad_shape = (
        jax.ShapeDtypeStruct((chunk, channels), F32)
        if spread
        else jax.ShapeDtypeStruct((hidden_width, channels), BF16)
    )
    others = max(replicas - 1, 1) if spread else 1
    slots = replicas if spread else 1
    vmem = pl.BlockSpec(memory_space=pltpu.VMEM)
    hbm = pl.BlockSpec(memory_space=pl.ANY)
    native = (micro_count, rows, width)
    stored, in_grad, out_grad, kernel_grad, gain_grad = pl.pallas_call(
        functools.partial(step_kernel, sections, replicas, spread, channels, mean_scale),
        out_shape=(
            jax.ShapeDtypeStruct(native, BF16),
            grad_shape,
            grad_shape,
            jax.ShapeDtypeStruct((KS * KS, channels), F32),
            jax.ShapeDtypeStruct((1, channels), F32),
        ),
        in_specs=[hbm, hbm, vmem, vmem, vmem, vmem],
        out_specs=(vmem,) * 5,
        scratch_shapes=[
            pltpu.VMEM(native, BF16),
            pltpu.VMEM(native, BF16),
            pltpu.VMEM(native, BF16),
            pltpu.VMEM((hidden_width, 384), BF16),
            pltpu.VMEM((hidden_width, 384), BF16),
            pltpu.VMEM((5, KS * KS, 8, LANES), F32),
            pltpu.VMEM((56, 384), F32),
            pltpu.VMEM((8, 384), F32),
            pltpu.VMEM((micro_count, pixels, hidden_width), BF16),
            pltpu.VMEM((micro_count, pixels, hidden_width), F32),
            pltpu.VMEM((micro_count, pixels, hidden_width), BF16),
            pltpu.VMEM((micro_count, pixels, 384), BF16),
            pltpu.VMEM((micro_count, pixels, 384), BF16),
            pltpu.VMEM((micro_count, pixels, 384), F32),
            pltpu.VMEM((micro_count, pixels, LANES), F32),
            pltpu.VMEM((micro_count, 5, pairs + 2 * REACH, rows + 16, LANES), F32),
            pltpu.VMEM((micro_count, 5, pairs, rows, LANES), F32),
            pltpu.VMEM((5, pairs, rows, LANES), F32),
            pltpu.VMEM((5, KS * KS, 8, LANES), F32),
            pltpu.VMEM((8, 384), F32),
            pltpu.VMEM((2, hidden_width, channels), BF16),
            pltpu.VMEM((2, others, chunk if spread else 16, channels), BF16),
            pltpu.VMEM((80, 384), BF16),
            pltpu.VMEM((slots, 80, 384), BF16),
            pltpu.SemaphoreType.DMA((2, micro_count)),
            pltpu.SemaphoreType.DMA((micro_count,)),
            pltpu.SemaphoreType.DMA((micro_count,)),
            pltpu.SemaphoreType.DMA((micro_count,)),
            pltpu.SemaphoreType.DMA((micro_count,)),
            pltpu.SemaphoreType.DMA((2, others)),
            pltpu.SemaphoreType.DMA((2, others)),
            pltpu.SemaphoreType.DMA((others,)),
            pltpu.SemaphoreType.DMA((others,)),
        ],
        compiler_params=pltpu.CompilerParams(
            collective_id=0, has_side_effects=True, vmem_limit_bytes=58 * 1024 * 1024
        ),
    )(
        images.reshape(native),
        cotangent.reshape(native),
        in_weight[0],
        out_weight[0],
        depth_kernel[0],
        norm_gain,
    )
    if not spread:
        in_grad, out_grad = (
            lax.psum_scatter(grad, "dp", scatter_dimension=0, tiled=True).astype(F32)
            for grad in (in_grad, out_grad)
        )
        kernel_grad, gain_grad = (
            lax.psum(grad.astype(BF16), "dp").astype(F32) for grad in (kernel_grad, gain_grad)
        )
    return (
        stored.reshape((1,) + images.shape),
        in_grad[None],
        out_grad[None],
        kernel_grad[None],
        gain_grad,
    )


def solution(mesh):
    placed = (
        P(None, ("groups", "dp"), None, None),
        P(None, ("groups", "dp"), None, None),
        P("section", None, None),
        P("section", None, None),
        P("section", None, None),
        P("section", None),
    )
    return jax.shard_map(
        local,
        mesh=mesh,
        in_specs=placed,
        out_specs=(
            P("section", None, ("groups", "dp"), None, None),
            P(("groups", "section"), "dp", None),
            P(("groups", "section"), "dp", None),
            P(("groups", "section"), None, None),
            P(("groups", "section"), None),
        ),
        check_vma=False,
    )
```

```python
import functools

import jax
import jax.numpy as jnp
from jax import lax
from jax.experimental import pallas as pl
from jax.experimental.pallas import tpu as pltpu
from jax.sharding import PartitionSpec as P

KS = 7
REACH = KS // 2
LANES = 128
MESH = pl.DeviceIdType.MESH

gelu_scale = 0.7978845608028654
cubic_term = 0.044715
norm_eps = 1e-06
F32 = jnp.float32
BF16 = jnp.bfloat16


def half_turn(tile):
    return pltpu.roll(tile, LANES // 2, axis=tile.ndim - 1)


def low_lanes(tile):
    return lax.broadcasted_iota(jnp.int32, tile.shape, tile.ndim - 1) < LANES // 2


def split_pair(tiles):
    t0, t1, t2, t3, t4 = tiles
    low = low_lanes(t0)
    q2, q3, q4 = half_turn(t2), half_turn(t3), half_turn(t4)
    first = (t0, t1, jnp.where(low, t2, 0.0))
    second = (jnp.where(low, q2, q3), jnp.where(low, q3, q4), jnp.where(low, q4, 0.0))
    return first, second


def merge_pair(first, second):
    low = low_lanes(first[0])
    q0, q1, q2 = (half_turn(t) for t in second)
    return (
        first[0],
        first[1],
        jnp.where(low, first[2], q0),
        jnp.where(low, q0, q1),
        jnp.where(low, q1, q2),
    )


def lane_tiles(value):
    return tuple(value[:, k * LANES : (k + 1) * LANES] for k in range(value.shape[1] // LANES))


def from_native(ref, slot):
    rows, width = ref.shape[1], ref.shape[2]
    parts = []
    for pair in range(width // (5 * LANES)):
        value = ref[slot, :, pair * 5 * LANES : (pair + 1) * 5 * LANES].astype(F32)
        first, second = split_pair(lane_tiles(value))
        parts.append(jnp.concatenate(first, axis=1))
        parts.append(jnp.concatenate(second, axis=1))
    return jnp.concatenate(parts, axis=0)


def to_native(ref, slot, value):
    rows, width = ref.shape[1], ref.shape[2]
    for pair in range(width // (5 * LANES)):
        first = lane_tiles(value[2 * pair * rows : (2 * pair + 1) * rows])
        second = lane_tiles(value[(2 * pair + 1) * rows : (2 * pair + 2) * rows])
        for k, tile in enumerate(merge_pair(first, second)):
            at = (pair * 5 + k) * LANES
            ref[slot, :, at : at + LANES] = tile.astype(ref.dtype)


def put_padded(field, slot, value, rows):
    half = value.shape[0] // 2
    pairs = half // rows
    left, right = lane_tiles(value[:half]), lane_tiles(value[half:])
    body = merge_pair(left, right)
    edge = REACH * rows
    zeros = tuple(jnp.zeros((edge, LANES), F32) for _ in range(3))
    before = merge_pair(zeros, lane_tiles(value[half - edge : half]))
    after = lane_tiles(value[half : half + edge])
    for k in range(5):
        field[slot, k, REACH : REACH + pairs, 8 : 8 + rows, :] = body[k].reshape(pairs, rows, LANES)
        if k >= 2:
            field[slot, k, 0:REACH, 8 : 8 + rows, :] = before[k].reshape(REACH, rows, LANES)
        if k <= 2:
            field[slot, k, REACH + pairs :, 8 : 8 + rows, :] = after[k].reshape(REACH, rows, LANES)
    return body


def convolve(field, slot, taps, out, flip):
    pairs, rows = out.shape[1], out.shape[2]

    def one_tile(k, carry):
        for part in range(rows // 8):
            total = jnp.zeros((pairs, 8, LANES), F32)
            for i in range(KS):
                window = field[slot, k, :, 8 - REACH + i + 8 * part : 16 - REACH + i + 8 * part, :]
                for j in range(KS):
                    tap = KS * i + j
                    tap = KS * KS - 1 - tap if flip else tap
                    total = total + window[j : j + pairs] * taps[k, tap][None]
            out[k, :, 8 * part : 8 * part + 8, :] = total
        return carry

    lax.fori_loop(0, 5, one_tile, 0)
    tiles = tuple(out[k].reshape(pairs * rows, LANES) for k in range(5))
    first, second = split_pair(tiles)
    return jnp.concatenate(
        [jnp.concatenate(first, axis=1), jnp.concatenate(second, axis=1)], axis=0
    )


def tap_terms(field, slot, kept, sums):
    pairs, rows = kept.shape[2], kept.shape[3]

    def one_tile(k, carry):
        for i in range(KS):
            windows = [
                field[slot, k, :, 8 - REACH + i + 8 * part : 16 - REACH + i + 8 * part, :]
                for part in range(rows // 8)
            ]
            for j in range(KS):
                total = None
                for part in range(rows // 8):
                    term = jnp.sum(
                        windows[part][j : j + pairs]
                        * kept[slot, k, :, 8 * part : 8 * part + 8, :],
                        axis=0,
                    )
                    total = term if total is None else total + term
                tap = KS * KS - 1 - (KS * i + j)
                sums[k, tap] = sums[k, tap] + total
        return carry

    lax.fori_loop(0, 5, one_tile, 0)


def step_kernel(
    sections, replicas, spread, channels, mean_scale,
    images, cotangent, weight_in, weight_out, kernel, gain,
    stored, in_grad, out_grad, kernel_grad, gain_grad,
    x_in, x_out, g_in, win, wout, taps, wide, gain_wide,
    hidden, slope, act_grad, normed, upstream, unit, inv_std,
    field, kept, conv, tap_sums, gain_sums, sent, landed, small, small_in,
    load_sem, weight_sem, fwd_send, fwd_recv, bwd_send, bwd_recv, sum_send, sum_recv, small_send, small_recv,
):
    me = lax.axis_index("section")
    replica = lax.axis_index("dp")
    last = sections - 1
    micro_count, rows, width = x_in.shape
    hidden_width = weight_in.shape[1]
    step = 256
    chunks = hidden_width // step
    pixels = rows * (width // channels)

    barrier = pltpu.get_barrier_semaphore()

    @pl.when(me > 0)
    def _():
        pl.semaphore_signal(barrier, inc=1, device_id={"section": me - 1}, device_id_type=MESH)

    @pl.when(me < last)
    def _():
        pl.semaphore_signal(barrier, inc=1, device_id={"section": me + 1}, device_id_type=MESH)

    if spread:
        for k in range(1, replicas):
            pl.semaphore_signal(
                barrier, inc=1,
                device_id={"dp": lax.rem(replica + k, replicas)}, device_id_type=MESH,
            )

    def load(source, target, m, which):
        return pltpu.make_async_copy(source.at[m], target.at[m], load_sem.at[which, m])

    weight_copies = tuple(
        pltpu.make_async_copy(source, target.at[0:channels, :], weight_sem.at[k])
        for k, (source, target) in enumerate(((weight_in, win), (weight_out, wout)))
    )
    for copy in weight_copies:
        copy.start()

    for m in range(micro_count):
        @pl.when(me == 0)
        def _():
            load(images, x_in, m, 0).start()

        @pl.when(me == last)
        def _():
            load(cotangent, g_in, m, 1).start()

    win[channels:384, :] = jnp.zeros((384 - channels, hidden_width), BF16)
    wout[channels:384, :] = jnp.zeros((384 - channels, hidden_width), BF16)
    wide[...] = jnp.zeros(wide.shape, F32)
    gain_wide[...] = jnp.zeros(gain_wide.shape, F32)
    for t in range(KS * KS):
        wide[t : t + 1, 0:channels] = kernel[t]
    gain_wide[:, 0:channels] = jnp.broadcast_to(gain[...], (8, channels))
    row_tiles = lane_tiles(wide[...])
    for k, tile in enumerate(merge_pair(row_tiles, row_tiles)):
        for t in range(KS * KS):
            taps[k, t] = jnp.broadcast_to(tile[t : t + 1], (8, LANES))
    field[...] = jnp.zeros(field.shape, F32)
    tap_sums[...] = jnp.zeros(tap_sums.shape, F32)
    gain_sums[...] = jnp.zeros(gain_sums.shape, F32)
    gain_row = gain_wide[0:1, :]

    for copy in weight_copies:
        copy.wait()
    neighbours = jnp.where(me > 0, 1, 0) + jnp.where(me < last, 1, 0)
    if spread:
        neighbours = neighbours + replicas - 1
    pl.semaphore_wait(barrier, neighbours)

    real = lax.broadcasted_iota(jnp.int32, (pixels, 384), 1) < channels
    by_channel = (((1,), (1,)), ((), ()))
    by_pixel = (((0,), (0,)), ((), ()))

    def ahead(m):
        return pltpu.make_async_remote_copy(
            src_ref=x_out.at[m], dst_ref=x_in.at[m],
            send_sem=fwd_send.at[m], recv_sem=fwd_recv.at[m],
            device_id={"section": jnp.minimum(me + 1, last)}, device_id_type=MESH,
        )

    def back(m):
        return pltpu.make_async_remote_copy(
            src_ref=stored.at[m], dst_ref=g_in.at[m],
            send_sem=bwd_send.at[m], recv_sem=bwd_recv.at[m],
            device_id={"section": jnp.maximum(me - 1, 0)}, device_id_type=MESH,
        )

    def forward(m, carry):
        @pl.when(me == 0)
        def _():
            load(images, x_in, m, 0).wait()

        @pl.when(me > 0)
        def _():
            ahead(m).wait_recv()

        x = from_native(x_in, m)
        body = put_padded(field, m, x, rows)
        for k in range(5):
            kept[m, k] = body[k].reshape(kept.shape[2:])
        u = convolve(field, m, taps, conv, False)
        mean = jnp.sum(u, axis=1, keepdims=True) * (1.0 / channels)
        centred = jnp.where(real, u - mean, 0.0)
        variance = jnp.sum(centred * centred, axis=1, keepdims=True) * (1.0 / channels)
        inverse = lax.rsqrt(variance + norm_eps)
        nhat = centred * inverse
        unit[m] = nhat
        inv_std[m] = jnp.broadcast_to(inverse, (pixels, LANES))
        n = (nhat * gain_row).astype(BF16)
        normed[m] = n
        mixed = None
        for c in range(chunks):
            at = slice(c * step, (c + 1) * step)
            a = jnp.dot(n, win[:, at], preferred_element_type=F32)
            square = a * a
            t = jnp.tanh(a * (gelu_scale + (gelu_scale * cubic_term) * square))
            plus = 0.5 + 0.5 * t
            h = (a * plus).astype(BF16)
            hidden[m, :, at] = h
            slope[m, :, at] = plus + (a * (plus * (1.0 - t))) * (
                gelu_scale + (3.0 * gelu_scale * cubic_term) * square
            )
            term = lax.dot_general(h, wout[:, at], by_channel, preferred_element_type=F32)
            mixed = term if mixed is None else mixed + term

        @pl.when(me < last)
        def _():
            to_native(x_out, m, x + mixed)
            ahead(m).start()

        return carry

    lax.fori_loop(0, micro_count, forward, 0)

    def backward(m, carry):
        @pl.when(me == last)
        def _():
            load(cotangent, g_in, m, 1).wait()

        @pl.when(me < last)
        def _():
            back(m).wait_recv()

        g = from_native(g_in, m)
        gb = g.astype(BF16)
        upstream[m] = gb
        dn = None
        for c in range(chunks):
            at = slice(c * step, (c + 1) * step)
            hg = jnp.dot(gb, wout[:, at], preferred_element_type=F32)
            da = (hg * slope[m, :, at]).astype(BF16)
            act_grad[m, :, at] = da
            term = lax.dot_general(da, win[:, at], by_channel, preferred_element_type=F32)
            dn = term if dn is None else dn + term
        nhat = unit[m]
        along = dn * nhat
        gain_sums[...] = gain_sums[...] + jnp.sum(along.reshape(pixels // 8, 8, 384), axis=0)
        q = dn * gain_row
        first = jnp.sum(q, axis=1, keepdims=True) * (1.0 / channels)
        second = jnp.sum(along * gain_row, axis=1, keepdims=True) * (1.0 / channels)
        du = jnp.where(real, inv_std[m][:, 0:1] * (q - first - nhat * second), 0.0)
        put_padded(field, m, du, rows)
        to_native(stored, m, g + convolve(field, m, taps, conv, True))

        @pl.when(me > 0)
        def _():
            back(m).start()

        return carry

    lax.fori_loop(0, micro_count, backward, 0)

    half_chunk = hidden_width // replicas // 2

    def rows_of(dest):
        return pl.ds(pl.multiple_of(dest * half_chunk, 16), half_chunk)

    def stage_of(way, t):
        place = replica if way == 0 else replicas - 1 - replica
        far = replicas - 1 - t + place
        dest = far if way == 0 else replicas - 1 - far
        return place, jnp.clip(dest, 0, replicas - 1)

    def hop(way, w, dest, fresh):
        target = replica + 1 if way == 0 else replica - 1
        return pltpu.make_async_remote_copy(
            src_ref=sent.at[w, rows_of(dest), :] if fresh else landed.at[way, w, dest],
            dst_ref=landed.at[way, w, dest],
            send_sem=sum_send.at[way, w, dest], recv_sem=sum_recv.at[way, w, dest],
            device_id={"dp": jnp.clip(target, 0, replicas - 1)}, device_id_type=MESH,
        )

    def stage(w, t):
        for way in range(2):
            place, dest = stage_of(way, t)
            if t > 0:
                settle(way, w, t - 1)

            @pl.when(place == 0)
            def _():
                hop(way, w, dest, True).start()

            @pl.when(jnp.logical_and(place > 0, place <= t))
            def _():
                onward = hop(way, w, dest, False)
                onward.wait_recv()
                slot = landed.at[way, w, dest]
                own = sent[w, rows_of(dest), :]
                slot[...] = (slot[...].astype(F32) + own.astype(F32)).astype(BF16)
                onward.start()

    def settle(way, w, t):
        place, dest = stage_of(way, t)

        @pl.when(place <= t)
        def _():
            hop(way, w, dest, False).wait_send()

    def finish(w, target):
        for way, there in ((0, replica > 0), (1, replica < replicas - 1)):

            @pl.when(there)
            def _():
                hop(way, w, replica, False).wait_recv()
                own = sent.at[w, rows_of(replica), :]
                own[...] = (own[...].astype(F32) + landed[way, w, replica].astype(F32)).astype(BF16)

            settle(way, w, replicas - 2)
        first, second = split_pair(lane_tiles(sent[w, rows_of(replica), :].astype(F32)))
        target[0:half_chunk, :] = jnp.concatenate(first, axis=1)[:, 0:channels]
        target[half_chunk:, :] = jnp.concatenate(second, axis=1)[:, 0:channels]

    for w, (wide_side, thin_side) in enumerate(((hidden, upstream), (act_grad, normed))):
        total = jnp.concatenate(
            [
                lax.dot_general(
                    wide_side[:, :, c * step : (c + 1) * step].reshape(micro_count * pixels, step),
                    thin_side[...].reshape(micro_count * pixels, 384),
                    by_pixel, preferred_element_type=F32,
                )
                for c in range(chunks)
            ],
            axis=0,
        ) * mean_scale
        if spread:
            for dest in range(replicas):
                at = 2 * dest * half_chunk
                tiles = merge_pair(
                    lane_tiles(total[at : at + half_chunk]),
                    lane_tiles(total[at + half_chunk : at + 2 * half_chunk]),
                )
                for k, tile in enumerate(tiles):
                    sent[
                        w, dest * half_chunk : (dest + 1) * half_chunk, k * LANES : (k + 1) * LANES
                    ] = tile.astype(BF16)
            stage(w, 0)
        elif w == 0:
            out_grad[...] = total[:, 0:channels].astype(BF16)
        else:
            in_grad[...] = total[:, 0:channels].astype(BF16)

    def per_micro(m, carry):
        tap_terms(field, m, kept, tap_sums)
        return carry

    done = 0
    if spread:
        for t in range(1, replicas - 1):
            lax.fori_loop(done, min(t, micro_count), per_micro, 0)
            done = min(t, micro_count)
            for w in range(2):
                stage(w, t)
    lax.fori_loop(done, micro_count, per_micro, 0)

    sums = tuple(jnp.sum(tap_sums[k], axis=1) for k in range(5))
    first, second = split_pair(sums)
    both = (jnp.concatenate(first, axis=1) + jnp.concatenate(second, axis=1)) * mean_scale
    gains = jnp.sum(gain_sums[...], axis=0, keepdims=True) * mean_scale
    if not spread:
        for t in range(KS * KS):
            kernel_grad[t] = both[t : t + 1, 0:channels]
        gain_grad[...] = gains[:, 0:channels]
    else:
        small[...] = jnp.zeros(small.shape, BF16)
        small[0:64, :] = jnp.concatenate(
            [both, jnp.zeros((15, 384), F32)], axis=0
        ).astype(BF16)
        small[64:80, :] = jnp.broadcast_to(gains, (16, 384)).astype(BF16)

        def share_small(k):
            return pltpu.make_async_remote_copy(
                src_ref=small, dst_ref=small_in.at[replica],
                send_sem=small_send.at[k - 1], recv_sem=small_recv.at[k - 1],
                device_id={"dp": lax.rem(replica + k, replicas)}, device_id_type=MESH,
            )

        for k in range(1, replicas):
            share_small(k).start()
        small_in[replica] = small[...]
        finish(0, out_grad)
        finish(1, in_grad)
        for k in range(1, replicas):
            share_small(k).wait()
        total = small_in[0].astype(F32)
        for k in range(1, replicas):
            total = total + small_in[k].astype(F32)
        for t in range(KS * KS):
            kernel_grad[t] = total[t : t + 1, 0:channels]
        gain_grad[...] = total[64:65, 0:channels]

    def drain(m, carry):
        @pl.when(me < last)
        def _():
            ahead(m).wait_send()

        @pl.when(me > 0)
        def _():
            back(m).wait_send()

        return carry

    lax.fori_loop(0, micro_count, drain, 0)


def local(images, cotangent, in_weight, out_weight, depth_kernel, norm_gain):
    sections = lax.axis_size("section")
    replicas = lax.axis_size("dp")
    micro_count, batch, rows, width = images.shape
    hidden_width, channels = in_weight.shape[1:]
    columns = width // channels
    pixels = rows * columns
    pairs = columns // 2
    assert batch == 1 and channels == 320 and rows % 8 == 0
    mean_scale = 1.0 / (micro_count * batch * replicas)
    chunk = hidden_width // replicas
    spread = chunk % 32 == 0 and 1 < replicas <= 8
    grad_shape = (
        ((chunk, channels), F32) if spread else ((hidden_width, channels), BF16)
    )
    others = max(replicas - 1, 1) if spread else 1
    slots = replicas if spread else 1
    vmem = pl.BlockSpec(memory_space=pltpu.VMEM)
    hbm = pl.BlockSpec(memory_space=pl.ANY)
    native = (micro_count, rows, width)
    stored, in_grad, out_grad, kernel_grad, gain_grad = pl.pallas_call(
        functools.partial(step_kernel, sections, replicas, spread, channels, mean_scale),
        out_shape=(
            pltpu.VMEM(native, BF16),
            pltpu.VMEM(*grad_shape),
            pltpu.VMEM(*grad_shape),
            pltpu.VMEM((KS * KS, 1, channels), F32),
            pltpu.VMEM((1, channels), F32),
        ),
        in_specs=[hbm, hbm, hbm, hbm, vmem, vmem],
        out_specs=(vmem,) * 5,
        scratch_shapes=[
            pltpu.VMEM(native, BF16),
            pltpu.VMEM(native, BF16),
            pltpu.VMEM(native, BF16),
            pltpu.VMEM((384, hidden_width), BF16),
            pltpu.VMEM((384, hidden_width), BF16),
            pltpu.VMEM((5, KS * KS, 8, LANES), F32),
            pltpu.VMEM((56, 384), F32),
            pltpu.VMEM((8, 384), F32),
            pltpu.VMEM((micro_count, pixels, hidden_width), BF16),
            pltpu.VMEM((micro_count, pixels, hidden_width), F32),
            pltpu.VMEM((micro_count, pixels, hidden_width), BF16),
            pltpu.VMEM((micro_count, pixels, 384), BF16),
            pltpu.VMEM((micro_count, pixels, 384), BF16),
            pltpu.VMEM((micro_count, pixels, 384), F32),
            pltpu.VMEM((micro_count, pixels, LANES), F32),
            pltpu.VMEM((micro_count, 5, pairs + 2 * REACH, rows + 16, LANES), F32),
            pltpu.VMEM((micro_count, 5, pairs, rows, LANES), F32),
            pltpu.VMEM((5, pairs, rows, LANES), F32),
            pltpu.VMEM((5, KS * KS, 8, LANES), F32),
            pltpu.VMEM((8, 384), F32),
            pltpu.VMEM((2, hidden_width // 2, 2 * channels), BF16),
            pltpu.VMEM((2, 2, slots, chunk // 2 if spread else 16, 2 * channels), BF16),
            pltpu.VMEM((80, 384), BF16),
            pltpu.VMEM((slots, 80, 384), BF16),
            pltpu.SemaphoreType.DMA((2, micro_count)),
            pltpu.SemaphoreType.DMA((2,)),
            pltpu.SemaphoreType.DMA((micro_count,)),
            pltpu.SemaphoreType.DMA((micro_count,)),
            pltpu.SemaphoreType.DMA((micro_count,)),
            pltpu.SemaphoreType.DMA((micro_count,)),
            pltpu.SemaphoreType.DMA((2, 2, slots)),
            pltpu.SemaphoreType.DMA((2, 2, slots)),
            pltpu.SemaphoreType.DMA((others,)),
            pltpu.SemaphoreType.DMA((others,)),
        ],
        compiler_params=pltpu.CompilerParams(
            collective_id=0, has_side_effects=True, vmem_limit_bytes=52 * 1024 * 1024
        ),
    )(
        images.reshape(native),
        cotangent.reshape(native),
        jnp.swapaxes(in_weight[0], 0, 1),
        jnp.swapaxes(out_weight[0], 0, 1),
        jnp.swapaxes(depth_kernel, 0, 1),
        norm_gain,
    )
    kernel_grad = jnp.swapaxes(kernel_grad, 0, 1)
    if not spread:
        in_grad, out_grad = (
            lax.psum_scatter(grad, "dp", scatter_dimension=0, tiled=True).astype(F32)
            for grad in (in_grad, out_grad)
        )
        kernel_grad, gain_grad = (
            lax.psum(grad.astype(BF16), "dp").astype(F32) for grad in (kernel_grad, gain_grad)
        )
    return (
        stored.reshape((1,) + images.shape),
        in_grad[None],
        out_grad[None],
        kernel_grad,
        gain_grad,
    )


def solution(mesh):
    placed = (
        P(None, ("groups", "dp"), None, None),
        P(None, ("groups", "dp"), None, None),
        P("section", None, None),
        P("section", None, None),
        P("section", None, None),
        P("section", None),
    )
    return jax.shard_map(
        local,
        mesh=mesh,
        in_specs=placed,
        out_specs=(
            P("section", None, ("groups", "dp"), None, None),
            P(("groups", "section"), "dp", None),
            P(("groups", "section"), "dp", None),
            P(("groups", "section"), None, None),
            P(("groups", "section"), None),
        ),
        check_vma=False,
    )
```

```python
import functools

import jax
import jax.numpy as jnp
from jax import lax
from jax.experimental import pallas as pl
from jax.experimental.pallas import tpu as pltpu
from jax.sharding import PartitionSpec as P

KS = 7
REACH = KS // 2
LANES = 128
MESH = pl.DeviceIdType.MESH

gelu_scale = 0.7978845608028654
cubic_term = 0.044715
norm_eps = 1e-06
F32 = jnp.float32
BF16 = jnp.bfloat16


def half_turn(tile):
    return pltpu.roll(tile, LANES // 2, axis=tile.ndim - 1)


def low_lanes(tile):
    return lax.broadcasted_iota(jnp.int32, tile.shape, tile.ndim - 1) < LANES // 2


def split_pair(tiles):
    t0, t1, t2, t3, t4 = tiles
    low = low_lanes(t0)
    q2, q3, q4 = half_turn(t2), half_turn(t3), half_turn(t4)
    first = (t0, t1, jnp.where(low, t2, 0.0))
    second = (jnp.where(low, q2, q3), jnp.where(low, q3, q4), jnp.where(low, q4, 0.0))
    return first, second


def merge_pair(first, second):
    low = low_lanes(first[0])
    q0, q1, q2 = (half_turn(t) for t in second)
    return (
        first[0],
        first[1],
        jnp.where(low, first[2], q0),
        jnp.where(low, q0, q1),
        jnp.where(low, q1, q2),
    )


def lane_tiles(value):
    return tuple(value[:, k * LANES : (k + 1) * LANES] for k in range(value.shape[1] // LANES))


def from_native(ref, slot):
    rows, width = ref.shape[1], ref.shape[2]
    parts = []
    for pair in range(width // (5 * LANES)):
        value = ref[slot, :, pair * 5 * LANES : (pair + 1) * 5 * LANES].astype(F32)
        first, second = split_pair(lane_tiles(value))
        parts.append(jnp.concatenate(first, axis=1))
        parts.append(jnp.concatenate(second, axis=1))
    return jnp.concatenate(parts, axis=0)


def to_native(ref, slot, value):
    rows, width = ref.shape[1], ref.shape[2]
    for pair in range(width // (5 * LANES)):
        first = lane_tiles(value[2 * pair * rows : (2 * pair + 1) * rows])
        second = lane_tiles(value[(2 * pair + 1) * rows : (2 * pair + 2) * rows])
        for k, tile in enumerate(merge_pair(first, second)):
            at = (pair * 5 + k) * LANES
            ref[slot, :, at : at + LANES] = tile.astype(ref.dtype)


def put_padded(field, slot, value, rows):
    half = value.shape[0] // 2
    pairs = half // rows
    left, right = lane_tiles(value[:half]), lane_tiles(value[half:])
    body = merge_pair(left, right)
    edge = REACH * rows
    zeros = tuple(jnp.zeros((edge, LANES), F32) for _ in range(3))
    before = merge_pair(zeros, lane_tiles(value[half - edge : half]))
    after = lane_tiles(value[half : half + edge])
    for k in range(5):
        field[slot, k, REACH : REACH + pairs, 8 : 8 + rows, :] = body[k].reshape(pairs, rows, LANES)
        if k >= 2:
            field[slot, k, 0:REACH, 8 : 8 + rows, :] = before[k].reshape(REACH, rows, LANES)
        if k <= 2:
            field[slot, k, REACH + pairs :, 8 : 8 + rows, :] = after[k].reshape(REACH, rows, LANES)
    return body


def convolve(field, slot, taps, out, flip):
    pairs, rows = out.shape[1], out.shape[2]

    def one_tile(k, carry):
        total = jnp.zeros((pairs, rows, LANES), F32)
        for i in range(KS):
            window = field[slot, k, :, 8 - REACH + i : 8 - REACH + i + rows, :]
            for j in range(KS):
                tap = KS * i + j
                tap = KS * KS - 1 - tap if flip else tap
                total = total + window[j : j + pairs] * taps[k, tap][0:1][None]
        out[k] = total
        return carry

    lax.fori_loop(0, 5, one_tile, 0)
    tiles = tuple(out[k].reshape(pairs * rows, LANES) for k in range(5))
    first, second = split_pair(tiles)
    return jnp.concatenate(
        [jnp.concatenate(first, axis=1), jnp.concatenate(second, axis=1)], axis=0
    )


def tap_terms(field, slot, kept, sums):
    pairs, rows = kept.shape[2], kept.shape[3]

    def one_tile(k, carry):
        for i in range(KS):
            windows = [
                field[slot, k, :, 8 - REACH + i + 8 * part : 16 - REACH + i + 8 * part, :]
                for part in range(rows // 8)
            ]
            for j in range(KS):
                total = None
                for part in range(rows // 8):
                    term = jnp.sum(
                        windows[part][j : j + pairs]
                        * kept[slot, k, :, 8 * part : 8 * part + 8, :],
                        axis=0,
                    )
                    total = term if total is None else total + term
                tap = KS * KS - 1 - (KS * i + j)
                sums[k, tap] = sums[k, tap] + total
        return carry

    lax.fori_loop(0, 5, one_tile, 0)


def step_kernel(
    sections, replicas, spread, channels, mean_scale,
    images, cotangent, weight_in, weight_out, kernel, gain,
    stored, in_grad, out_grad, kernel_grad, gain_grad,
    x_in, x_out, g_in, win, wout, taps, wide, gain_wide,
    hidden, slope, act_grad, normed, upstream, unit, inv_std,
    field, kept, conv, tap_sums, gain_sums, sent, landed, small, small_in,
    load_sem, weight_sem, fwd_send, fwd_recv, bwd_send, bwd_recv, sum_send, sum_recv, small_send, small_recv,
):
    me = lax.axis_index("section")
    replica = lax.axis_index("dp")
    last = sections - 1
    micro_count, rows, width = x_in.shape
    hidden_width = weight_in.shape[1]
    step = 256
    chunks = hidden_width // step
    pixels = rows * (width // channels)

    barrier = pltpu.get_barrier_semaphore()

    @pl.when(me > 0)
    def _():
        pl.semaphore_signal(barrier, inc=1, device_id={"section": me - 1}, device_id_type=MESH)

    @pl.when(me < last)
    def _():
        pl.semaphore_signal(barrier, inc=1, device_id={"section": me + 1}, device_id_type=MESH)

    if spread:
        for k in range(1, replicas):
            pl.semaphore_signal(
                barrier, inc=1,
                device_id={"dp": lax.rem(replica + k, replicas)}, device_id_type=MESH,
            )

    def load(source, target, m, which):
        return pltpu.make_async_copy(source.at[m], target.at[m], load_sem.at[which, m])

    weight_copies = tuple(
        pltpu.make_async_copy(source, target.at[0:channels, :], weight_sem.at[k])
        for k, (source, target) in enumerate(((weight_in, win), (weight_out, wout)))
    )
    for copy in weight_copies:
        copy.start()

    for m in range(micro_count):
        @pl.when(me == 0)
        def _():
            load(images, x_in, m, 0).start()

        @pl.when(me == last)
        def _():
            load(cotangent, g_in, m, 1).start()

    win[channels:384, :] = jnp.zeros((384 - channels, hidden_width), BF16)
    wout[channels:384, :] = jnp.zeros((384 - channels, hidden_width), BF16)
    wide[...] = jnp.zeros(wide.shape, F32)
    gain_wide[...] = jnp.zeros(gain_wide.shape, F32)
    for t in range(KS * KS):
        wide[t : t + 1, 0:channels] = kernel[t]
    gain_wide[:, 0:channels] = jnp.broadcast_to(gain[...], (8, channels))
    row_tiles = lane_tiles(wide[...])
    for k, tile in enumerate(merge_pair(row_tiles, row_tiles)):
        for t in range(KS * KS):
            taps[k, t] = jnp.broadcast_to(tile[t : t + 1], (8, LANES))
    field[...] = jnp.zeros(field.shape, F32)
    tap_sums[...] = jnp.zeros(tap_sums.shape, F32)
    gain_sums[...] = jnp.zeros(gain_sums.shape, F32)
    gain_row = gain_wide[0:1, :]

    for copy in weight_copies:
        copy.wait()
    neighbours = jnp.where(me > 0, 1, 0) + jnp.where(me < last, 1, 0)
    if spread:
        neighbours = neighbours + replicas - 1
    pl.semaphore_wait(barrier, neighbours)

    real = lax.broadcasted_iota(jnp.int32, (pixels, 384), 1) < channels
    by_channel = (((1,), (1,)), ((), ()))
    by_pixel = (((0,), (0,)), ((), ()))

    def ahead(m):
        return pltpu.make_async_remote_copy(
            src_ref=x_out.at[m], dst_ref=x_in.at[m],
            send_sem=fwd_send.at[m], recv_sem=fwd_recv.at[m],
            device_id={"section": jnp.minimum(me + 1, last)}, device_id_type=MESH,
        )

    def back(m):
        return pltpu.make_async_remote_copy(
            src_ref=stored.at[m], dst_ref=g_in.at[m],
            send_sem=bwd_send.at[m], recv_sem=bwd_recv.at[m],
            device_id={"section": jnp.maximum(me - 1, 0)}, device_id_type=MESH,
        )

    def forward(m, carry):
        @pl.when(me == 0)
        def _():
            load(images, x_in, m, 0).wait()

        @pl.when(me > 0)
        def _():
            ahead(m).wait_recv()

        x = from_native(x_in, m)
        body = put_padded(field, m, x, rows)
        for k in range(5):
            kept[m, k] = body[k].reshape(kept.shape[2:])
        u = convolve(field, m, taps, conv, False)
        mean = jnp.sum(u, axis=1, keepdims=True) * (1.0 / channels)
        centred = jnp.where(real, u - mean, 0.0)
        variance = jnp.sum(centred * centred, axis=1, keepdims=True) * (1.0 / channels)
        inverse = lax.rsqrt(variance + norm_eps)
        nhat = centred * inverse
        unit[m] = nhat
        inv_std[m] = jnp.broadcast_to(inverse, (pixels, LANES))
        n = (nhat * gain_row).astype(BF16)
        normed[m] = n
        mixed = None
        for c in range(chunks):
            at = slice(c * step, (c + 1) * step)
            a = jnp.dot(n, win[:, at], preferred_element_type=F32)
            square = a * a
            t = jnp.tanh(a * (gelu_scale + (gelu_scale * cubic_term) * square))
            plus = 0.5 + 0.5 * t
            h = (a * plus).astype(BF16)
            hidden[m, :, at] = h
            slope[m, :, at] = plus + (a * (plus * (1.0 - t))) * (
                gelu_scale + (3.0 * gelu_scale * cubic_term) * square
            )
            term = lax.dot_general(h, wout[:, at], by_channel, preferred_element_type=F32)
            mixed = term if mixed is None else mixed + term

        @pl.when(me < last)
        def _():
            to_native(x_out, m, x + mixed)
            ahead(m).start()

        return carry

    lax.fori_loop(0, micro_count, forward, 0)

    def backward(m, carry):
        @pl.when(me == last)
        def _():
            load(cotangent, g_in, m, 1).wait()

        @pl.when(me < last)
        def _():
            back(m).wait_recv()

        g = from_native(g_in, m)
        gb = g.astype(BF16)
        upstream[m] = gb
        dn = None
        for c in range(chunks):
            at = slice(c * step, (c + 1) * step)
            hg = jnp.dot(gb, wout[:, at], preferred_element_type=F32)
            da = (hg * slope[m, :, at]).astype(BF16)
            act_grad[m, :, at] = da
            term = lax.dot_general(da, win[:, at], by_channel, preferred_element_type=F32)
            dn = term if dn is None else dn + term
        nhat = unit[m]
        along = dn * nhat
        gain_sums[...] = gain_sums[...] + jnp.sum(along.reshape(pixels // 8, 8, 384), axis=0)
        q = dn * gain_row
        first = jnp.sum(q, axis=1, keepdims=True) * (1.0 / channels)
        second = jnp.sum(along * gain_row, axis=1, keepdims=True) * (1.0 / channels)
        du = jnp.where(real, inv_std[m][:, 0:1] * (q - first - nhat * second), 0.0)
        put_padded(field, m, du, rows)
        to_native(stored, m, g + convolve(field, m, taps, conv, True))

        @pl.when(me > 0)
        def _():
            back(m).start()

        return carry

    lax.fori_loop(0, micro_count, backward, 0)

    half_chunk = hidden_width // replicas // 2

    def rows_of(dest):
        return pl.ds(pl.multiple_of(dest * half_chunk, 16), half_chunk)

    def stage_of(way, t):
        place = replica if way == 0 else replicas - 1 - replica
        far = replicas - 1 - t + place
        dest = far if way == 0 else replicas - 1 - far
        return place, jnp.clip(dest, 0, replicas - 1)

    def hop(way, w, dest, fresh):
        target = replica + 1 if way == 0 else replica - 1
        return pltpu.make_async_remote_copy(
            src_ref=sent.at[w, rows_of(dest), :] if fresh else landed.at[way, w, dest],
            dst_ref=landed.at[way, w, dest],
            send_sem=sum_send.at[way, w, dest], recv_sem=sum_recv.at[way, w, dest],
            device_id={"dp": jnp.clip(target, 0, replicas - 1)}, device_id_type=MESH,
        )

    def stage(w, t):
        for way in range(2):
            place, dest = stage_of(way, t)
            if t > 0:
                settle(way, w, t - 1)

            @pl.when(place == 0)
            def _():
                hop(way, w, dest, True).start()

            @pl.when(jnp.logical_and(place > 0, place <= t))
            def _():
                onward = hop(way, w, dest, False)
                onward.wait_recv()
                slot = landed.at[way, w, dest]
                own = sent[w, rows_of(dest), :]
                slot[...] = (slot[...].astype(F32) + own.astype(F32)).astype(BF16)
                onward.start()

    def settle(way, w, t):
        place, dest = stage_of(way, t)

        @pl.when(place <= t)
        def _():
            hop(way, w, dest, False).wait_send()

    def finish(w, target):
        for way, there in ((0, replica > 0), (1, replica < replicas - 1)):

            @pl.when(there)
            def _():
                hop(way, w, replica, False).wait_recv()
                own = sent.at[w, rows_of(replica), :]
                own[...] = (own[...].astype(F32) + landed[way, w, replica].astype(F32)).astype(BF16)

            settle(way, w, replicas - 2)
        first, second = split_pair(lane_tiles(sent[w, rows_of(replica), :].astype(F32)))
        target[0:half_chunk, :] = jnp.concatenate(first, axis=1)[:, 0:channels]
        target[half_chunk:, :] = jnp.concatenate(second, axis=1)[:, 0:channels]

    for w, (wide_side, thin_side) in enumerate(((hidden, upstream), (act_grad, normed))):
        total = jnp.concatenate(
            [
                lax.dot_general(
                    wide_side[:, :, c * step : (c + 1) * step].reshape(micro_count * pixels, step),
                    thin_side[...].reshape(micro_count * pixels, 384),
                    by_pixel, preferred_element_type=F32,
                )
                for c in range(chunks)
            ],
            axis=0,
        ) * mean_scale
        if spread:
            for dest in range(replicas):
                at = 2 * dest * half_chunk
                tiles = merge_pair(
                    lane_tiles(total[at : at + half_chunk]),
                    lane_tiles(total[at + half_chunk : at + 2 * half_chunk]),
                )
                for k, tile in enumerate(tiles):
                    sent[
                        w, dest * half_chunk : (dest + 1) * half_chunk, k * LANES : (k + 1) * LANES
                    ] = tile.astype(BF16)
            stage(w, 0)
        elif w == 0:
            out_grad[...] = total[:, 0:channels].astype(BF16)
        else:
            in_grad[...] = total[:, 0:channels].astype(BF16)

    def per_micro(m, carry):
        tap_terms(field, m, kept, tap_sums)
        return carry

    done = 0
    if spread:
        for t in range(1, replicas - 1):
            lax.fori_loop(done, min(t, micro_count), per_micro, 0)
            done = min(t, micro_count)
            for w in range(2):
                stage(w, t)
    lax.fori_loop(done, micro_count, per_micro, 0)

    sums = tuple(jnp.sum(tap_sums[k], axis=1) for k in range(5))
    first, second = split_pair(sums)
    both = (jnp.concatenate(first, axis=1) + jnp.concatenate(second, axis=1)) * mean_scale
    gains = jnp.sum(gain_sums[...], axis=0, keepdims=True) * mean_scale
    if not spread:
        for t in range(KS * KS):
            kernel_grad[t] = both[t : t + 1, 0:channels]
        gain_grad[...] = gains[:, 0:channels]
    else:
        small[...] = jnp.zeros(small.shape, BF16)
        small[0:64, :] = jnp.concatenate(
            [both, jnp.zeros((15, 384), F32)], axis=0
        ).astype(BF16)
        small[64:80, :] = jnp.broadcast_to(gains, (16, 384)).astype(BF16)

        def share_small(k):
            return pltpu.make_async_remote_copy(
                src_ref=small, dst_ref=small_in.at[replica],
                send_sem=small_send.at[k - 1], recv_sem=small_recv.at[k - 1],
                device_id={"dp": lax.rem(replica + k, replicas)}, device_id_type=MESH,
            )

        for k in range(1, replicas):
            share_small(k).start()
        small_in[replica] = small[...]
        finish(0, out_grad)
        finish(1, in_grad)
        for k in range(1, replicas):
            share_small(k).wait()
        total = small_in[0].astype(F32)
        for k in range(1, replicas):
            total = total + small_in[k].astype(F32)
        for t in range(KS * KS):
            kernel_grad[t] = total[t : t + 1, 0:channels]
        gain_grad[...] = total[64:65, 0:channels]

    def drain(m, carry):
        @pl.when(me < last)
        def _():
            ahead(m).wait_send()

        @pl.when(me > 0)
        def _():
            back(m).wait_send()

        return carry

    lax.fori_loop(0, micro_count, drain, 0)


def local(images, cotangent, in_weight, out_weight, depth_kernel, norm_gain):
    sections = lax.axis_size("section")
    replicas = lax.axis_size("dp")
    micro_count, batch, rows, width = images.shape
    hidden_width, channels = in_weight.shape[1:]
    columns = width // channels
    pixels = rows * columns
    pairs = columns // 2
    assert batch == 1 and channels == 320 and rows % 8 == 0
    mean_scale = 1.0 / (micro_count * batch * replicas)
    chunk = hidden_width // replicas
    spread = chunk % 32 == 0 and 1 < replicas <= 8
    grad_shape = (
        ((chunk, channels), F32) if spread else ((hidden_width, channels), BF16)
    )
    others = max(replicas - 1, 1) if spread else 1
    slots = replicas if spread else 1
    vmem = pl.BlockSpec(memory_space=pltpu.VMEM)
    hbm = pl.BlockSpec(memory_space=pl.ANY)
    native = (micro_count, rows, width)
    stored, in_grad, out_grad, kernel_grad, gain_grad = pl.pallas_call(
        functools.partial(step_kernel, sections, replicas, spread, channels, mean_scale),
        out_shape=(
            pltpu.VMEM(native, BF16),
            pltpu.VMEM(*grad_shape),
            pltpu.VMEM(*grad_shape),
            pltpu.VMEM((KS * KS, 1, channels), F32),
            pltpu.VMEM((1, channels), F32),
        ),
        in_specs=[hbm, hbm, hbm, hbm, vmem, vmem],
        out_specs=(vmem,) * 5,
        scratch_shapes=[
            pltpu.VMEM(native, BF16),
            pltpu.VMEM(native, BF16),
            pltpu.VMEM(native, BF16),
            pltpu.VMEM((384, hidden_width), BF16),
            pltpu.VMEM((384, hidden_width), BF16),
            pltpu.VMEM((5, KS * KS, 8, LANES), F32),
            pltpu.VMEM((56, 384), F32),
            pltpu.VMEM((8, 384), F32),
            pltpu.VMEM((micro_count, pixels, hidden_width), BF16),
            pltpu.VMEM((micro_count, pixels, hidden_width), F32),
            pltpu.VMEM((micro_count, pixels, hidden_width), BF16),
            pltpu.VMEM((micro_count, pixels, 384), BF16),
            pltpu.VMEM((micro_count, pixels, 384), BF16),
            pltpu.VMEM((micro_count, pixels, 384), F32),
            pltpu.VMEM((micro_count, pixels, LANES), F32),
            pltpu.VMEM((micro_count, 5, pairs + 2 * REACH, rows + 16, LANES), F32),
            pltpu.VMEM((micro_count, 5, pairs, rows, LANES), F32),
            pltpu.VMEM((5, pairs, rows, LANES), F32),
            pltpu.VMEM((5, KS * KS, 8, LANES), F32),
            pltpu.VMEM((8, 384), F32),
            pltpu.VMEM((2, hidden_width // 2, 2 * channels), BF16),
            pltpu.VMEM((2, 2, slots, chunk // 2 if spread else 16, 2 * channels), BF16),
            pltpu.VMEM((80, 384), BF16),
            pltpu.VMEM((slots, 80, 384), BF16),
            pltpu.SemaphoreType.DMA((2, micro_count)),
            pltpu.SemaphoreType.DMA((2,)),
            pltpu.SemaphoreType.DMA((micro_count,)),
            pltpu.SemaphoreType.DMA((micro_count,)),
            pltpu.SemaphoreType.DMA((micro_count,)),
            pltpu.SemaphoreType.DMA((micro_count,)),
            pltpu.SemaphoreType.DMA((2, 2, slots)),
            pltpu.SemaphoreType.DMA((2, 2, slots)),
            pltpu.SemaphoreType.DMA((others,)),
            pltpu.SemaphoreType.DMA((others,)),
        ],
        compiler_params=pltpu.CompilerParams(
            collective_id=0, has_side_effects=True, vmem_limit_bytes=52 * 1024 * 1024
        ),
    )(
        images.reshape(native),
        cotangent.reshape(native),
        jnp.swapaxes(in_weight[0], 0, 1),
        jnp.swapaxes(out_weight[0], 0, 1),
        jnp.swapaxes(depth_kernel, 0, 1),
        norm_gain,
    )
    kernel_grad = jnp.swapaxes(kernel_grad, 0, 1)
    if not spread:
        in_grad, out_grad = (
            lax.psum_scatter(grad, "dp", scatter_dimension=0, tiled=True).astype(F32)
            for grad in (in_grad, out_grad)
        )
        kernel_grad, gain_grad = (
            lax.psum(grad.astype(BF16), "dp").astype(F32) for grad in (kernel_grad, gain_grad)
        )
    return (
        stored.reshape((1,) + images.shape),
        in_grad[None],
        out_grad[None],
        kernel_grad,
        gain_grad,
    )


def solution(mesh):
    placed = (
        P(None, ("groups", "dp"), None, None),
        P(None, ("groups", "dp"), None, None),
        P("section", None, None),
        P("section", None, None),
        P("section", None, None),
        P("section", None),
    )
    return jax.shard_map(
        local,
        mesh=mesh,
        in_specs=placed,
        out_specs=(
            P("section", None, ("groups", "dp"), None, None),
            P(("groups", "section"), "dp", None),
            P(("groups", "section"), "dp", None),
            P(("groups", "section"), None, None),
            P(("groups", "section"), None),
        ),
        check_vma=False,
    )
```
